32 devices in a mesh: row: 4 (over z), col: 8 (over y, x, core).
Axes of the slice: x: 2, y: 2, z: 4, core: 2. Of those that a mesh axis runs over, the one named last changes fastest.
Arguments:
- embeddings: bfloat16 [4096, 768], P(('row', 'col')), may hold values from -4 to 4
- neg_ids: int32 [4, 2048], P('row', 'col'), may hold values from 0 to 16383, as said below
- neg_counts: int32 [4], P('row'), may hold values from 256 to 2048, as said below
- index_rows: bfloat16 [16384, 768], P('row'), may hold values from -4 to 4
Outputs:
- row_loss: float32 [4096], P(('row', 'col'))
- grad: float32 [4096, 768], P(('row', 'col'))
The draws below stay inside these ranges and needn't reach their ends.
Inputs may be any that keep to these rules, and one draw needn't show every extreme that they name: `neg_counts`: every entry lies within the range; some lists are full (2048) and some hold exactly 256 entries. Index shard of an id is id // 4096. Among the 256 slots of one device (neg_ids[b, c * 256 : (c + 1) * 256]) at most 128 ids belong to any one index shard, and in every such run exactly 128 belong to one of them.
All inputs are finite; a program needn't handle non-finite values.
Results may differ from the reference program's by a relative error of at most 0.00059.
Values may be sent and summed in bfloat16 or wider, within the bound.
A program may use at most 128 MiB of HBM per device.

```python
import jax
import jax.numpy as jnp
from jax import lax

D = 768
HN_DEV = 256
IDX_DEV = 4096
BLOCKS = 4
BATCH = 4096
HMAX = 2048
NIDX = 16384


def aligned_rows(key):
    k_one, k_two, k_three, k_four = jax.random.split(jax.random.fold_in(key, 31), 4)
    offset = jax.random.randint(k_one, (), 0, 64)
    rows = jnp.arange(BATCH, dtype=jnp.int32)
    chosen = (rows + offset) % 64 == 0
    signs = jnp.where(jax.random.bernoulli(k_two, 0.5, (1, D)), 1.0, -1.0)
    strength = jax.random.uniform(k_three, (BATCH, 1), jnp.float32, 3.6, 3.8)
    noise = jax.random.uniform(k_four, (BATCH, D), jnp.float32, -0.2, 0.2)
    aligned = jnp.clip(strength * signs + noise, -4.0, 4.0)
    return (chosen, aligned)


def draw_embeddings(key, part):
    k_two = jax.random.fold_in(key, 1)
    chosen, aligned = aligned_rows(key)
    base = jnp.clip(jax.random.normal(k_two, (BATCH, D), jnp.float32), -4.0, 4.0)
    return jnp.where(chosen[:, None], aligned, base).astype(jnp.bfloat16)


def draw_neg_counts(key, part):
    k_one, k_two, k_three = jax.random.split(jax.random.fold_in(key, 11), 3)
    counts = jax.random.randint(k_one, (BLOCKS,), HN_DEV, HMAX + 1)
    fullest = jax.random.randint(k_two, (), 0, BLOCKS)
    emptiest = (fullest + 1 + jax.random.randint(k_three, (), 0, BLOCKS - 1)) % BLOCKS
    blocks = jnp.arange(BLOCKS, dtype=jnp.int32)
    counts = jnp.where(blocks == fullest, HMAX, counts)
    counts = jnp.where(blocks == emptiest, HN_DEV, counts)
    return counts.astype(jnp.int32)


def draw_neg_ids(key, part):
    shards = NIDX // IDX_DEV
    runs = HMAX // HN_DEV
    bound = 2 * HN_DEV // shards
    keys = jax.random.split(jax.random.fold_in(key, 23), BLOCKS * runs)

    def one_run(run_key):
        k_one, k_two, k_three = jax.random.split(run_key, 3)
        heavy = jax.random.randint(k_one, (), 0, shards)
        slots = jnp.arange(HN_DEV, dtype=jnp.int32)
        other = (heavy + 1 + (slots - bound) % (shards - 1)) % shards
        owners = jnp.where(slots < bound, heavy, other)
        owners = owners[jax.random.permutation(k_two, HN_DEV)]
        local = jax.random.randint(k_three, (HN_DEV,), 0, IDX_DEV)
        return (owners * IDX_DEV + local).astype(jnp.int32)
    return jax.vmap(one_run)(keys).reshape(BLOCKS, HMAX)


def block_levels(stream_key, dims, cuts, low, high):
    loudness = 1.0
    for dim, shards_of in cuts:
        heights = jax.random.uniform(jax.random.fold_in(jax.random.fold_in(stream_key, 6), dim), (shards_of,), jnp.float32, low / len(cuts), high / len(cuts))
        loudness = loudness * jnp.repeat(jnp.exp(heights), dims[dim] // shards_of).reshape((-1,) + (1,) * (len(dims) - 1 - dim))
    return loudness


def normal_values(stream_key, extent, scale, most, cuts=(), kind=jnp.bfloat16):
    drawn = scale * jax.random.normal(stream_key, extent, jnp.float32)
    if cuts:
        drawn = drawn * block_levels(stream_key, extent, cuts, -0.22, 0.18)
    return jnp.clip(drawn, -most, most).astype(kind)


def setup_inputs(seed: int = 0) -> dict:
    streams_of = jax.random.split(jax.random.key(seed), 5)
    return {
        "embeddings": draw_embeddings(jax.random.fold_in(streams_of[4], 71), 0),
        "neg_ids": draw_neg_ids(jax.random.fold_in(streams_of[4], 71), 0),
        "neg_counts": draw_neg_counts(jax.random.fold_in(streams_of[4], 71), 0),
        "index_rows": normal_values(streams_of[3], (NIDX, D), 1.0, 4.0, ((0, 4),)),
    }


def reference(embeddings, neg_ids, neg_counts, index_rows):
    scale = D ** -0.5
    block_rows = BATCH // BLOCKS
    every = jnp.arange(BATCH, dtype=jnp.int32)
    slots = jnp.arange(HMAX, dtype=jnp.int32)

    def one_block(carry, block):
        start = (block * block_rows).astype(jnp.int32)
        rows = lax.dynamic_slice_in_dim(embeddings, start, block_rows, 0)
        listed = lax.dynamic_index_in_dim(neg_ids, block, 0, keepdims=False)
        count = lax.dynamic_index_in_dim(neg_counts, block, 0, keepdims=False)
        negatives = jnp.take(index_rows, listed, axis=0)
        glob = start + jnp.arange(block_rows, dtype=jnp.int32)
        scores = jnp.dot(rows, embeddings.T, preferred_element_type=jnp.float32) * scale
        scores = jnp.where(glob[:, None] == every[None, :], -jnp.inf, scores)
        hard = jnp.dot(rows, negatives.T, preferred_element_type=jnp.float32) * scale
        hard = jnp.where((slots < count)[None, :], hard, -jnp.inf)
        top = jnp.maximum(jnp.max(scores, axis=1), jnp.max(hard, axis=1))
        total = jnp.sum(jnp.exp(scores - top[:, None]), axis=1) + jnp.sum(jnp.exp(hard - top[:, None]), axis=1)
        lse = top + jnp.log(total)
        rows_f = rows.astype(jnp.float32)
        partner = rows_f.reshape(block_rows // 2, 2, D)[:, ::-1].reshape(block_rows, D)
        positive = jnp.sum(rows_f * partner, axis=1) * scale
        loss = lse - positive
        target = (jnp.bitwise_xor(glob, 1)[:, None] == every[None, :]).astype(jnp.float32)
        probs_grad = (jnp.exp(scores - lse[:, None]) - target).astype(jnp.bfloat16)
        hard_probs = jnp.exp(hard - lse[:, None]).astype(jnp.bfloat16)
        row_term = jnp.dot(probs_grad, embeddings, preferred_element_type=jnp.float32)
        row_term = row_term + jnp.dot(hard_probs, negatives, preferred_element_type=jnp.float32)
        carry = carry + lax.dot_general(probs_grad, rows, (((0,), (0,)), ((), ())), preferred_element_type=jnp.float32)
        return carry, (loss, row_term)

    init = jnp.zeros((BATCH, D), jnp.float32)
    col_terms, outs = lax.scan(one_block, init, jnp.arange(BLOCKS, dtype=jnp.int32))
    row_loss = outs[0].reshape(BATCH)
    grad = outs[1].reshape(BATCH, D) + col_terms
    return row_loss, grad
```

```python
import functools

import jax
import jax.numpy as jnp
from jax import lax
from jax.experimental import pallas as pl
from jax.experimental.pallas import tpu as pltpu
from jax.sharding import PartitionSpec as P

D = 768
F32 = jnp.float32
BF16 = jnp.bfloat16
NT = (((1,), (1,)), ((), ()))
TN = (((0,), (0,)), ((), ()))


def kernel(n_row, n_col, cap, emb, ids, cnt, index, loss, grad,
           q, kn, s, sel, cid_s, cid_r, idx_v, hot, ng_s, ng_r, st_s, st_r, lk_s, lk_r,
           sib_s, sib_r, keep, red_s, red_r,
           idx_sem, cid_ss, cid_rs, k_ss, k_rs, q_ss, q_rs, ng_ss, ng_rs, st_ss, st_rs,
           lk_ss, lk_rs, sib_ss, sib_rs, red_ss, red_rs):
    scale = D ** (-0.5)
    n_chip = n_col // 2
    rows = emb.shape[0]
    slots = ids.shape[1]
    owned = index.shape[0]
    n_key = n_row * rows
    r = lax.axis_index("row")
    c = lax.axis_index("col")
    chip = c // 2
    core = c % 2

    def row_peer(e):
        return (lax.rem(r + e, n_row), c)

    def col_peer(m, b):
        other = core if b == 0 else 1 - core
        return (r, lax.rem(chip + m, n_chip) * 2 + other)

    def remote(src, dst, send_sem, recv_sem, device):
        return pltpu.make_async_remote_copy(
            src_ref=src, dst_ref=dst, send_sem=send_sem, recv_sem=recv_sem,
            device_id=device, device_id_type=pl.DeviceIdType.MESH)

    col_steps = [(m, b) for m in range(n_chip) for b in range(2) if m or b]

    def mirror(m, b):
        return 2 * ((n_chip - m) % n_chip) + b

    load = pltpu.make_async_copy(index, idx_v, idx_sem)
    load.start()
    barrier = pltpu.get_barrier_semaphore()
    for e in range(1, n_row):
        pl.semaphore_signal(barrier, inc=1, device_id=row_peer(e),
                            device_id_type=pl.DeviceIdType.MESH)
    for m, b in col_steps:
        pl.semaphore_signal(barrier, inc=1, device_id=col_peer(m, b),
                            device_id_type=pl.DeviceIdType.MESH)

    listed = ids[...]
    masks, locals_ = [], []
    for e in range(n_row):
        local = listed - lax.rem(r + e, n_row) * owned
        masks.append(jnp.where((local >= 0) & (local < owned), 1.0, 0.0).astype(F32))
        locals_.append(local)
    before = (lax.broadcasted_iota(jnp.int32, (slots, slots), 0)
              < lax.broadcasted_iota(jnp.int32, (slots, slots), 1))
    mask = jnp.concatenate(masks, axis=0)
    rank = jnp.dot(mask.astype(BF16), jnp.where(before, 1.0, 0.0).astype(BF16),
                   preferred_element_type=F32)
    place = lax.broadcasted_iota(jnp.int32, (128, slots), 0).astype(F32)
    line = lax.broadcasted_iota(jnp.int32, (8, slots), 0)
    for e in range(n_row):
        chosen = jnp.where((place == rank[e:e + 1, :]) & (masks[e] > 0.5), 1.0, 0.0)
        sel[e * cap:(e + 1) * cap, :] = chosen[:cap].astype(BF16)
        local = jnp.where(masks[e] > 0.5, locals_[e], 0)
        high = jnp.right_shift(local, 6).astype(F32)
        low = jnp.bitwise_and(local, 63).astype(F32)
        parts = jnp.where(line == 0, high, jnp.where(line == 1, low, 1.0))
        got = lax.dot_general(parts.astype(BF16), chosen.astype(BF16), NT,
                              preferred_element_type=F32)
        packed = jnp.where(got[2:3] > 0.5, got[0:1] * 64.0 + got[1:2], -1.0)
        wide = jnp.broadcast_to(packed, (8, 128))
        if e == 0:
            cid_r[0] = wide
        else:
            cid_s[e] = wide

    pl.semaphore_wait(barrier, n_row - 1 + len(col_steps))
    cid_copies, k_copies, q_copies = {}, {}, {}
    for e in range(1, n_row):
        back = n_row - e
        cid_copies[e] = remote(cid_s.at[e], cid_r.at[back], cid_ss.at[e], cid_rs.at[back],
                               row_peer(e))
        cid_copies[e].start()
    for e in range(1, n_row):
        back = n_row - e
        k_copies[e] = remote(emb, kn.at[pl.ds(back * rows, rows)], k_ss.at[e], k_rs.at[back],
                             row_peer(e))
        k_copies[e].start()
    own_rows = pl.ds(pl.multiple_of(core * rows, rows), rows)
    for m, b in col_steps:
        q_copies[m, b] = remote(emb, q.at[chip, own_rows], q_ss.at[2 * m + b],
                                q_rs.at[mirror(m, b)], col_peer(m, b))
        q_copies[m, b].start()
    kn[0:rows, :] = emb[...]
    q[chip, own_rows, :] = emb[...]

    columns = []
    for e in range(n_row):
        if e:
            remote(cid_s.at[e], cid_r.at[e], cid_ss.at[e], cid_rs.at[e], row_peer(e)).wait_recv()
        columns.append(jnp.broadcast_to(cid_r[e][0:1, :], (128, 128)).T[:cap])
    wanted = jnp.concatenate(columns, axis=0)
    lane = lax.broadcasted_iota(jnp.int32, (n_row * cap, 128), 1).astype(F32)
    for j in range(owned // 128):
        hot[:, j * 128:(j + 1) * 128] = jnp.where(
            wanted == lane + float(j * 128), 1.0, 0.0).astype(BF16)
    load.wait()
    for j in range(D // 256):
        part = pl.ds(j * 256, 256)
        picked = jnp.dot(hot[...], idx_v[:, part], preferred_element_type=F32).astype(BF16)
        ng_r[0:cap, part] = picked[:cap]
        ng_s[:, part] = picked
    ng_copies = {}
    for e in range(1, n_row):
        back = n_row - e
        ng_copies[e] = remote(ng_s.at[pl.ds(e * cap, cap)], ng_r.at[pl.ds(back * cap, cap)],
                              ng_ss.at[e], ng_rs.at[back], row_peer(e))
        ng_copies[e].start()

    for e in range(1, n_row):
        remote(emb, kn.at[pl.ds(e * rows, rows)], k_ss.at[e], k_rs.at[e], row_peer(e)).wait_recv()
    own = lax.broadcasted_iota(jnp.int32, (rows, 2 * rows), 0)
    other = lax.broadcasted_iota(jnp.int32, (rows, 2 * rows), 1) - core * rows
    same = own == other
    partner = jnp.bitwise_xor(own, 1) == other
    positive = None
    for m in range(n_chip):
        at = lax.rem(chip + m, n_chip)
        for b in range(2):
            if m or b:
                remote(emb, q.at[at, pl.ds(pl.multiple_of((core if b == 0 else 1 - core) * rows, rows), rows)],
                       q_ss.at[2 * m + b], q_rs.at[2 * m + b], col_peer(m, b)).wait_recv()
        block = lax.dot_general(kn[0:n_key, :], q[at], NT, preferred_element_type=F32) * scale
        if m == 0:
            first = block[0:rows]
            positive = jnp.sum(jnp.where(partner, first, 0.0), axis=0, keepdims=True)
            s[at, 0:rows, :] = jnp.where(same, -jnp.inf, first)
            s[at, rows:n_key, :] = block[rows:]
        else:
            s[at, 0:n_key, :] = block

    for e in range(1, n_row):
        remote(ng_s.at[pl.ds(e * cap, cap)], ng_r.at[pl.ds(e * cap, cap)], ng_ss.at[e],
               ng_rs.at[e], row_peer(e)).wait_recv()
    kn[n_key:n_key + slots, :] = lax.dot_general(
        sel[...], ng_r[...], TN, preferred_element_type=F32).astype(BF16)
    live = (lax.broadcasted_iota(jnp.int32, (slots, 2 * rows), 0) + c * slots) < cnt[0]
    for m in range(n_chip):
        at = lax.rem(chip + m, n_chip)
        hard = lax.dot_general(kn[n_key:n_key + slots, :], q[at], NT,
                               preferred_element_type=F32) * scale
        hard = jnp.where(live, hard, -jnp.inf)
        s[at, n_key:n_key + slots, :] = hard
        block = s[at, 0:n_key, :]
        top = jnp.maximum(jnp.max(block, axis=0, keepdims=True),
                          jnp.max(hard, axis=0, keepdims=True))
        total = (jnp.sum(jnp.exp(block - top), axis=0, keepdims=True)
                 + jnp.sum(jnp.exp(hard - top), axis=0, keepdims=True))
        st_s[at, 0:1, :] = top
        st_s[at, 1:2, :] = total
    st_copies = {}
    for m, b in col_steps:
        st_copies[m, b] = remote(st_s, st_r.at[mirror(m, b)], st_ss.at[2 * m + b],
                                 st_rs.at[mirror(m, b)], col_peer(m, b))
        st_copies[m, b].start()
    for m, b in col_steps:
        remote(st_s, st_r.at[2 * m + b], st_ss.at[2 * m + b], st_rs.at[2 * m + b],
               col_peer(m, b)).wait_recv()

    def lse_of(at):
        tops = [st_s[at, 0:1, :]] + [st_r[2 * m + b, at, 0:1, :] for m, b in col_steps]
        sums = [st_s[at, 1:2, :]] + [st_r[2 * m + b, at, 1:2, :] for m, b in col_steps]
        top = functools.reduce(jnp.maximum, tops)
        return top + jnp.log(sum(v * jnp.exp(t - top) for t, v in zip(tops, sums)))

    own_lse = lse_of(chip)
    both = jnp.concatenate([own_lse, own_lse - positive], axis=0)
    half = jnp.where(core == 0, both[:, 0:rows], both[:, rows:2 * rows])
    loss[...] = half[1:2]
    mine = jnp.broadcast_to(half[0:1], (8, rows))
    lk_s[...] = mine
    lk_copies = {}
    for e in range(1, n_row):
        back = n_row - e
        lk_copies[e] = remote(lk_s, lk_r.at[back], lk_ss.at[e], lk_rs.at[back], row_peer(e))
        lk_copies[e].start()
    key_lse = [jnp.broadcast_to(half[0:1], (rows, rows)).T]
    for e in range(1, n_row):
        remote(lk_s, lk_r.at[e], lk_ss.at[e], lk_rs.at[e], row_peer(e)).wait_recv()
        key_lse.append(jnp.broadcast_to(lk_r[e][0:1, :], (rows, rows)).T)
    key_lse = jnp.concatenate(key_lse, axis=0)
    key_lse = jnp.concatenate([key_lse, key_lse], axis=1)

    sib_copies, red_copies = {}, {}
    sibling = col_peer(0, 1)

    def pass_on(m):
        sib_copies[m].wait_recv()
        red_s[m] = keep[m] + sib_r[m]
        back = n_chip - m
        red_copies[m] = remote(red_s.at[m], red_r.at[back], red_ss.at[m], red_rs.at[back],
                               col_peer(m, 0))
        red_copies[m].start()

    order = list(range(1, n_chip)) + [0]
    for n, m in enumerate(order):
        at = lax.rem(chip + m, n_chip)
        lse = own_lse if m == 0 else lse_of(at)
        as_query = jnp.exp(s[at] - lse)
        as_key = jnp.exp(s[at, 0:n_key, :] - key_lse)
        if m == 0:
            target = jnp.where(partner, 1.0, 0.0)
            as_query = jnp.concatenate([as_query[0:rows] - target, as_query[rows:]], axis=0)
            as_key = jnp.concatenate([as_key[0:rows] - target, as_key[rows:]], axis=0)
        term = lax.dot_general(as_query.astype(BF16), kn[...], TN, preferred_element_type=F32)
        term += lax.dot_general(as_key.astype(BF16), kn[0:n_key, :], TN,
                                preferred_element_type=F32)
        keep[m] = jnp.where(core == 0, term[0:rows], term[rows:])
        sib_s[m] = jnp.where(core == 0, term[rows:], term[0:rows])
        sib_copies[m] = remote(sib_s.at[m], sib_r.at[m], sib_ss.at[m], sib_rs.at[m], sibling)
        sib_copies[m].start()
        if n >= 1:
            pass_on(order[n - 1])
    sib_copies[0].wait_recv()
    total = keep[0] + sib_r[0]
    for m in range(1, n_chip):
        remote(red_s.at[m], red_r.at[m], red_ss.at[m], red_rs.at[m], col_peer(m, 0)).wait_recv()
        total += red_r[m]
    grad[...] = total

    for copies in (cid_copies, k_copies, q_copies, ng_copies, st_copies, lk_copies,
                   sib_copies, red_copies):
        for copy in copies.values():
            copy.wait_send()


def per_device(n_row, n_col, embeddings, neg_ids, neg_counts, index_rows):
    rows = embeddings.shape[0]
    slots = neg_ids.shape[1]
    owned = index_rows.shape[0]
    cap = 2 * slots // n_row
    n_chip = n_col // 2
    n_key = n_row * rows
    vmem = pltpu.VMEM
    dma = pltpu.SemaphoreType.DMA
    loss, grad = pl.pallas_call(
        functools.partial(kernel, n_row, n_col, cap),
        out_shape=(jax.ShapeDtypeStruct((1, rows), F32),
                   jax.ShapeDtypeStruct((rows, D), F32)),
        in_specs=[pl.BlockSpec(memory_space=vmem), pl.BlockSpec(memory_space=vmem),
                  pl.BlockSpec(memory_space=pltpu.SMEM), pl.BlockSpec(memory_space=pl.ANY)],
        out_specs=(pl.BlockSpec(memory_space=vmem), pl.BlockSpec(memory_space=vmem)),
        scratch_shapes=[
            vmem((n_chip, 2 * rows, D), BF16),
            vmem((n_key + slots, D), BF16),
            vmem((n_chip, n_key + slots, 2 * rows), F32),
            vmem((n_row * cap, slots), BF16),
            vmem((n_row, 8, 128), F32),
            vmem((n_row, 8, 128), F32),
            vmem((owned, D), BF16),
            vmem((n_row * cap, owned), BF16),
            vmem((n_row * cap, D), BF16),
            vmem((n_row * cap, D), BF16),
            vmem((n_chip, 2, 2 * rows), F32),
            vmem((n_col, n_chip, 2, 2 * rows), F32),
            vmem((8, rows), F32),
            vmem((n_row, 8, rows), F32),
            vmem((n_chip, rows, D), F32),
            vmem((n_chip, rows, D), F32),
            vmem((n_chip, rows, D), F32),
            vmem((n_chip, rows, D), F32),
            vmem((n_chip, rows, D), F32),
            dma,
            dma((n_row,)), dma((n_row,)), dma((n_row,)), dma((n_row,)),
            dma((n_col,)), dma((n_col,)), dma((n_row,)), dma((n_row,)),
            dma((n_col,)), dma((n_col,)), dma((n_row,)), dma((n_row,)),
            dma((n_chip,)), dma((n_chip,)), dma((n_chip,)), dma((n_chip,)),
        ],
        compiler_params=pltpu.CompilerParams(
            collective_id=0, has_side_effects=True, vmem_limit_bytes=58 * 1024 * 1024),
    )(embeddings, neg_ids, neg_counts, index_rows)
    return loss.reshape(rows), grad


def solution(mesh):
    return jax.shard_map(
        functools.partial(per_device, mesh.shape["row"], mesh.shape["col"]),
        mesh=mesh,
        in_specs=(P(("row", "col"), None), P("row", "col"), P("row"), P("row", None)),
        out_specs=(P(("row", "col")), P(("row", "col"), None)),
        check_vma=False,
    )
```

```python
import functools

import jax
import jax.numpy as jnp
from jax import lax
from jax.experimental import pallas as pl
from jax.experimental.pallas import tpu as pltpu
from jax.sharding import PartitionSpec as P

D = 768
F32 = jnp.float32
BF16 = jnp.bfloat16
NT = (((1,), (1,)), ((), ()))
TN = (((0,), (0,)), ((), ()))


def kernel(n_row, n_col, cap, emb, ids, cnt, index, loss, grad,
           q, kn, s, sel, cid_s, cid_r, idx_v, hot, ng_s, ng_r, st_s, st_r, lk_s, lk_r,
           sib_s, sib_r, keep, red_s, red_r, unit_s, unit_r, acc,
           idx_sem, cid_ss, cid_rs, k_ss, k_rs, q_ss, q_rs, ng_ss, ng_rs, st_ss, st_rs,
           lk_ss, lk_rs, sib_ss, sib_rs, red_ss, red_rs, unit_ss, unit_rs):
    scale = D ** (-0.5)
    n_chip = n_col // 2
    rows = emb.shape[0]
    slots = ids.shape[1]
    owned = index.shape[0]
    n_key = n_row * rows
    r = lax.axis_index("row")
    c = lax.axis_index("col")
    chip = c // 2
    core = c % 2

    def row_peer(e):
        return (lax.rem(r + e, n_row), c)

    def col_peer(m, b):
        other = core if b == 0 else 1 - core
        return (r, lax.rem(chip + m, n_chip) * 2 + other)

    def remote(src, dst, send_sem, recv_sem, device):
        return pltpu.make_async_remote_copy(
            src_ref=src, dst_ref=dst, send_sem=send_sem, recv_sem=recv_sem,
            device_id=device, device_id_type=pl.DeviceIdType.MESH)

    col_steps = [(m, b) for m in range(n_chip) for b in range(2) if m or b]

    def mirror(m, b):
        return 2 * ((n_chip - m) % n_chip) + b

    load = pltpu.make_async_copy(index, idx_v, idx_sem)
    load.start()
    barrier = pltpu.get_barrier_semaphore()
    for e in range(1, n_row):
        pl.semaphore_signal(barrier, inc=1, device_id=row_peer(e),
                            device_id_type=pl.DeviceIdType.MESH)
    for m, b in col_steps:
        pl.semaphore_signal(barrier, inc=1, device_id=col_peer(m, b),
                            device_id_type=pl.DeviceIdType.MESH)

    listed = ids[...]
    masks, locals_ = [], []
    for e in range(n_row):
        local = listed - lax.rem(r + e, n_row) * owned
        masks.append(jnp.where((local >= 0) & (local < owned), 1.0, 0.0).astype(F32))
        locals_.append(local)
    before = (lax.broadcasted_iota(jnp.int32, (slots, slots), 0)
              < lax.broadcasted_iota(jnp.int32, (slots, slots), 1))
    mask = jnp.concatenate(masks, axis=0)
    rank = jnp.dot(mask.astype(BF16), jnp.where(before, 1.0, 0.0).astype(BF16),
                   preferred_element_type=F32)
    place = lax.broadcasted_iota(jnp.int32, (128, slots), 0).astype(F32)
    line = lax.broadcasted_iota(jnp.int32, (8, slots), 0)
    for e in range(n_row):
        chosen = jnp.where((place == rank[e:e + 1, :]) & (masks[e] > 0.5), 1.0, 0.0)
        sel[e * cap:(e + 1) * cap, :] = chosen[:cap].astype(BF16)
        local = jnp.where(masks[e] > 0.5, locals_[e], 0)
        high = jnp.right_shift(local, 6).astype(F32)
        low = jnp.bitwise_and(local, 63).astype(F32)
        parts = jnp.where(line == 0, high, jnp.where(line == 1, low, 1.0))
        got = lax.dot_general(parts.astype(BF16), chosen.astype(BF16), NT,
                              preferred_element_type=F32)
        packed = jnp.where(got[2:3] > 0.5, got[0:1] * 64.0 + got[1:2], -1.0)
        wide = jnp.broadcast_to(packed, (8, 128))
        if e == 0:
            cid_r[0] = wide
        else:
            cid_s[e] = wide

    pl.semaphore_wait(barrier, n_row - 1 + len(col_steps))
    cid_copies, q_copies = {}, {}

    def key_slot(owner):
        return kn.at[pl.ds(pl.multiple_of(owner * rows, rows), rows)]

    def key_copy(way, h):
        step = 1 if way == 0 else -1
        owner = r - step * (h - 1)
        src = emb if h == 1 else key_slot(owner)
        return remote(src, key_slot(owner), k_ss.at[way, h], k_rs.at[way, h], (r + step, c))

    def sends(way, h):
        return (r + 1 < n_row) & (r >= h - 1) if way == 0 else (r >= 1) & (r + h - 1 < n_row)

    def key_send(h):
        for way in range(2):
            @pl.when(sends(way, h))
            def _():
                key_copy(way, h).start()

    def key_sent(h):
        for way in range(2):
            @pl.when(sends(way, h))
            def _():
                key_copy(way, h).wait_send()

    def key_wait(h):
        for way in range(2):
            @pl.when((r >= h) if way == 0 else (r + h < n_row))
            def _():
                owner = r - h if way == 0 else r + h
                remote(emb, key_slot(owner), k_ss.at[way, h], k_rs.at[way, h],
                       row_peer(1)).wait_recv()

    for e in range(1, n_row):
        back = n_row - e
        cid_copies[e] = remote(cid_s.at[e], cid_r.at[back], cid_ss.at[e], cid_rs.at[back],
                               row_peer(e))
        cid_copies[e].start()
    key_send(1)
    own_rows = pl.ds(pl.multiple_of(core * rows, rows), rows)
    for m, b in col_steps:
        q_copies[m, b] = remote(emb, q.at[chip, own_rows], q_ss.at[2 * m + b],
                                q_rs.at[mirror(m, b)], col_peer(m, b))
        q_copies[m, b].start()
    kn[pl.ds(pl.multiple_of(r * rows, rows), rows), :] = emb[...]
    q[chip, own_rows, :] = emb[...]

    columns = []
    for e in range(n_row):
        if e:
            remote(cid_s.at[e], cid_r.at[e], cid_ss.at[e], cid_rs.at[e], row_peer(e)).wait_recv()
        columns.append(jnp.broadcast_to(cid_r[e][0:1, :], (128, 128)).T[:cap])
    wanted = jnp.concatenate(columns, axis=0)
    lane = lax.broadcasted_iota(jnp.int32, (n_row * cap, 128), 1).astype(F32)
    for j in range(owned // 128):
        hot[:, j * 128:(j + 1) * 128] = jnp.where(
            wanted == lane + float(j * 128), 1.0, 0.0).astype(BF16)
    load.wait()
    for j in range(D // 256):
        part = pl.ds(j * 256, 256)
        picked = jnp.dot(hot[...], idx_v[:, part], preferred_element_type=F32).astype(BF16)
        ng_r[0:cap, part] = picked[:cap]
        ng_s[:, part] = picked
    if n_row > 2:
        key_wait(1)
        key_send(2)
    ng_copies = {}
    for e in range(1, n_row):
        back = n_row - e
        ng_copies[e] = remote(ng_s.at[pl.ds(e * cap, cap)], ng_r.at[pl.ds(back * cap, cap)],
                              ng_ss.at[e], ng_rs.at[back], row_peer(e))
        ng_copies[e].start()

    for h in range(2, n_row - 1):
        key_wait(h)
        key_send(h + 1)
    key_wait(n_row - 1)
    own = lax.broadcasted_iota(jnp.int32, (n_key, 2 * rows), 0) - r * rows
    other = lax.broadcasted_iota(jnp.int32, (n_key, 2 * rows), 1) - core * rows
    other = jnp.where((other >= 0) & (other < rows), other, 2 * n_key)
    same = own == other
    partner = jnp.bitwise_xor(own, 1) == other
    positive = None
    for m in range(n_chip):
        at = lax.rem(chip + m, n_chip)
        for b in range(2):
            if m or b:
                remote(emb, q.at[at, pl.ds(pl.multiple_of((core if b == 0 else 1 - core) * rows, rows), rows)],
                       q_ss.at[2 * m + b], q_rs.at[2 * m + b], col_peer(m, b)).wait_recv()
        block = lax.dot_general(kn[0:n_key, :], q[at], NT, preferred_element_type=F32) * scale
        if m == 0:
            positive = jnp.sum(jnp.where(partner, block, 0.0), axis=0, keepdims=True)
            block = jnp.where(same, -jnp.inf, block)
        s[at, 0:n_key, :] = block

    for e in range(1, n_row):
        remote(ng_s.at[pl.ds(e * cap, cap)], ng_r.at[pl.ds(e * cap, cap)], ng_ss.at[e],
               ng_rs.at[e], row_peer(e)).wait_recv()
    kn[n_key:n_key + slots, :] = lax.dot_general(
        sel[...], ng_r[...], TN, preferred_element_type=F32).astype(BF16)
    live = (lax.broadcasted_iota(jnp.int32, (slots, 2 * rows), 0) + c * slots) < cnt[0]
    for m in range(n_chip):
        at = lax.rem(chip + m, n_chip)
        hard = lax.dot_general(kn[n_key:n_key + slots, :], q[at], NT,
                               preferred_element_type=F32) * scale
        hard = jnp.where(live, hard, -jnp.inf)
        s[at, n_key:n_key + slots, :] = hard
        block = s[at, 0:n_key, :]
        top = jnp.maximum(jnp.max(block, axis=0, keepdims=True),
                          jnp.max(hard, axis=0, keepdims=True))
        total = (jnp.sum(jnp.exp(block - top), axis=0, keepdims=True)
                 + jnp.sum(jnp.exp(hard - top), axis=0, keepdims=True))
        st_s[at, 0:1, :] = top
        st_s[at, 1:2, :] = total
    st_copies = {}
    for m, b in col_steps:
        st_copies[m, b] = remote(st_s, st_r.at[mirror(m, b)], st_ss.at[2 * m + b],
                                 st_rs.at[mirror(m, b)], col_peer(m, b))
        st_copies[m, b].start()
    for m, b in col_steps:
        remote(st_s, st_r.at[2 * m + b], st_ss.at[2 * m + b], st_rs.at[2 * m + b],
               col_peer(m, b)).wait_recv()

    def lse_of(at):
        tops = [st_s[at, 0:1, :]] + [st_r[2 * m + b, at, 0:1, :] for m, b in col_steps]
        sums = [st_s[at, 1:2, :]] + [st_r[2 * m + b, at, 1:2, :] for m, b in col_steps]
        top = functools.reduce(jnp.maximum, tops)
        return top + jnp.log(sum(v * jnp.exp(t - top) for t, v in zip(tops, sums)))

    own_lse = lse_of(chip)
    both = jnp.concatenate([own_lse, own_lse - positive], axis=0)
    half = jnp.where(core == 0, both[:, 0:rows], both[:, rows:2 * rows])
    loss[...] = half[1:2]
    mine = jnp.broadcast_to(half[0:1], (8, rows))
    lk_s[...] = mine
    lk_r[r] = mine
    lk_copies = {}
    for e in range(1, n_row):
        lk_copies[e] = remote(lk_s, lk_r.at[r], lk_ss.at[e], lk_rs.at[n_row - e], row_peer(e))
        lk_copies[e].start()

    def query_term(m):
        at = lax.rem(chip + m, n_chip)
        weight = jnp.exp(s[at] - (own_lse if m == 0 else lse_of(at)))
        if m == 0:
            weight = jnp.concatenate(
                [weight[0:n_key] - jnp.where(partner, 1.0, 0.0), weight[n_key:]], axis=0)
        return lax.dot_general(weight.astype(BF16), kn[...], TN, preferred_element_type=F32)

    def key_term(m):
        weight = jnp.exp(s[lax.rem(chip + m, n_chip), 0:n_key, :] - key_lse)
        if m == 0:
            weight = weight - jnp.where(partner, 1.0, 0.0)
        return lax.dot_general(weight.astype(BF16), kn[0:n_key, :], TN,
                               preferred_element_type=F32)

    order = list(range(1, n_chip)) + [0]
    early = order[:2]
    for n, m in enumerate(early):
        acc[n] = query_term(m)
    key_lse = []
    for e in range(1, n_row):
        remote(lk_s, lk_r.at[lax.rem(r + e, n_row)], lk_ss.at[e], lk_rs.at[e],
               row_peer(e)).wait_recv()
    for e in range(n_row):
        key_lse.append(jnp.broadcast_to(lk_r[e][0:1, :], (rows, rows)).T)
    key_lse = jnp.concatenate(key_lse, axis=0)
    key_lse = jnp.concatenate([key_lse, key_lse], axis=1)

    sib_copies, red_copies, unit_copies = {}, {}, {}
    sibling = col_peer(0, 1)

    def pass_on(m):
        sib_copies[m].wait_recv()
        both_sum = keep[m] + sib_r[m]
        largest = jnp.maximum(jnp.max(jnp.abs(both_sum), axis=1, keepdims=True), 1e-30)
        unit = largest * (1.0 / 32000.0)
        steps = jnp.round(both_sum * (1.0 / unit))
        red_s[m] = steps.astype(jnp.int32).astype(jnp.int16)
        unit_s[m] = jnp.broadcast_to(unit, (rows, 128)).T[0:8]
        back = n_chip - m
        red_copies[m] = remote(red_s.at[m], red_r.at[back], red_ss.at[m], red_rs.at[back],
                               col_peer(m, 0))
        red_copies[m].start()
        unit_copies[m] = remote(unit_s.at[m], unit_r.at[back], unit_ss.at[m], unit_rs.at[back],
                                col_peer(m, 0))
        unit_copies[m].start()

    for n, m in enumerate(order):
        term = acc[n] + key_term(m) if m in early else query_term(m) + key_term(m)
        keep[m] = jnp.where(core == 0, term[0:rows], term[rows:])
        sib_s[m] = jnp.where(core == 0, term[rows:], term[0:rows])
        sib_copies[m] = remote(sib_s.at[m], sib_r.at[m], sib_ss.at[m], sib_rs.at[m], sibling)
        sib_copies[m].start()
        if n >= 1:
            pass_on(order[n - 1])
    sib_copies[0].wait_recv()
    total = keep[0] + sib_r[0]
    for m in range(1, n_chip):
        remote(red_s.at[m], red_r.at[m], red_ss.at[m], red_rs.at[m], col_peer(m, 0)).wait_recv()
        remote(unit_s.at[m], unit_r.at[m], unit_ss.at[m], unit_rs.at[m],
               col_peer(m, 0)).wait_recv()
        unit = jnp.broadcast_to(unit_r[m][0:1, :], (128, rows)).T[:, 0:1]
        total += red_r[m].astype(jnp.int32).astype(F32) * unit
    grad[...] = total

    for h in range(1, n_row):
        key_sent(h)
    for copies in (cid_copies, q_copies, ng_copies, st_copies, lk_copies,
                   sib_copies, red_copies, unit_copies):
        for copy in copies.values():
            copy.wait_send()


def per_device(n_row, n_col, embeddings, neg_ids, neg_counts, index_rows):
    rows = embeddings.shape[0]
    slots = neg_ids.shape[1]
    owned = index_rows.shape[0]
    cap = 2 * slots // n_row
    n_chip = n_col // 2
    n_key = n_row * rows
    vmem = pltpu.VMEM
    dma = pltpu.SemaphoreType.DMA
    loss, grad = pl.pallas_call(
        functools.partial(kernel, n_row, n_col, cap),
        out_shape=(jax.ShapeDtypeStruct((1, rows), F32),
                   jax.ShapeDtypeStruct((rows, D), F32)),
        in_specs=[pl.BlockSpec(memory_space=vmem), pl.BlockSpec(memory_space=vmem),
                  pl.BlockSpec(memory_space=pltpu.SMEM), pl.BlockSpec(memory_space=pl.ANY)],
        out_specs=(pl.BlockSpec(memory_space=vmem), pl.BlockSpec(memory_space=vmem)),
        scratch_shapes=[
            vmem((n_chip, 2 * rows, D), BF16),
            vmem((n_key + slots, D), BF16),
            vmem((n_chip, n_key + slots, 2 * rows), F32),
            vmem((n_row * cap, slots), BF16),
            vmem((n_row, 8, 128), F32),
            vmem((n_row, 8, 128), F32),
            vmem((owned, D), BF16),
            vmem((n_row * cap, owned), BF16),
            vmem((n_row * cap, D), BF16),
            vmem((n_row * cap, D), BF16),
            vmem((n_chip, 2, 2 * rows), F32),
            vmem((n_col, n_chip, 2, 2 * rows), F32),
            vmem((8, rows), F32),
            vmem((n_row, 8, rows), F32),
            vmem((n_chip, rows, D), F32),
            vmem((n_chip, rows, D), F32),
            vmem((n_chip, rows, D), F32),
            vmem((n_chip, rows, D), jnp.int16),
            vmem((n_chip, rows, D), jnp.int16),
            vmem((n_chip, 8, rows), F32),
            vmem((n_chip, 8, rows), F32),
            vmem((2, 2 * rows, D), F32),
            dma,
            dma((n_row,)), dma((n_row,)), dma((2, n_row)), dma((2, n_row)),
            dma((n_col,)), dma((n_col,)), dma((n_row,)), dma((n_row,)),
            dma((n_col,)), dma((n_col,)), dma((n_row,)), dma((n_row,)),
            dma((n_chip,)), dma((n_chip,)), dma((n_chip,)), dma((n_chip,)),
            dma((n_chip,)), dma((n_chip,)),
        ],
        compiler_params=pltpu.CompilerParams(
            collective_id=0, has_side_effects=True, vmem_limit_bytes=58 * 1024 * 1024),
    )(embeddings, neg_ids, neg_counts, index_rows)
    return loss.reshape(rows), grad


def solution(mesh):
    return jax.shard_map(
        functools.partial(per_device, mesh.shape["row"], mesh.shape["col"]),
        mesh=mesh,
        in_specs=(P(("row", "col"), None), P("row", "col"), P("row"), P("row", None)),
        out_specs=(P(("row", "col")), P(("row", "col"), None)),
        check_vma=False,
    )
```

```python
import functools

import jax
import jax.numpy as jnp
from jax import lax
from jax.experimental import pallas as pl
from jax.experimental.pallas import tpu as pltpu
from jax.sharding import PartitionSpec as P

D = 768
F32 = jnp.float32
BF16 = jnp.bfloat16
NT = (((1,), (1,)), ((), ()))
TN = (((0,), (0,)), ((), ()))


def kernel(n_row, n_col, cap, emb, ids, cnt, index, loss, grad,
           q, kn, s, sel, cid_s, cid_r, idx_v, hot, ng_s, ng_r, st_s, st_r, lk_s, lk_r,
           sib_s, sib_r, keep, red_s, red_r, unit_s, unit_r, acc,
           idx_sem, cid_ss, cid_rs, k_ss, k_rs, q_ss, q_rs, ng_ss, ng_rs, st_ss, st_rs,
           lk_ss, lk_rs, sib_ss, sib_rs, red_ss, red_rs, unit_ss, unit_rs):
    scale = D ** (-0.5)
    n_chip = n_col // 2
    rows = emb.shape[0]
    slots = ids.shape[1]
    owned = index.shape[0]
    n_key = n_row * rows
    r = lax.axis_index("row")
    c = lax.axis_index("col")
    chip = c // 2
    core = c % 2

    def row_peer(e):
        return (lax.rem(r + e, n_row), c)

    def col_peer(m, b):
        other = core if b == 0 else 1 - core
        return (r, lax.rem(chip + m, n_chip) * 2 + other)

    def remote(src, dst, send_sem, recv_sem, device):
        return pltpu.make_async_remote_copy(
            src_ref=src, dst_ref=dst, send_sem=send_sem, recv_sem=recv_sem,
            device_id=device, device_id_type=pl.DeviceIdType.MESH)

    col_steps = [(m, b) for m in range(n_chip) for b in range(2) if m or b]

    def mirror(m, b):
        return 2 * ((n_chip - m) % n_chip) + b

    load = pltpu.make_async_copy(index, idx_v, idx_sem)
    load.start()
    barrier = pltpu.get_barrier_semaphore()
    for e in range(1, n_row):
        pl.semaphore_signal(barrier, inc=1, device_id=row_peer(e),
                            device_id_type=pl.DeviceIdType.MESH)
    for m, b in col_steps:
        pl.semaphore_signal(barrier, inc=1, device_id=col_peer(m, b),
                            device_id_type=pl.DeviceIdType.MESH)

    listed = ids[...]
    masks, locals_ = [], []
    for e in range(n_row):
        local = listed - lax.rem(r + e, n_row) * owned
        masks.append(jnp.where((local >= 0) & (local < owned), 1.0, 0.0).astype(F32))
        locals_.append(local)
    before = (lax.broadcasted_iota(jnp.int32, (slots, slots), 0)
              < lax.broadcasted_iota(jnp.int32, (slots, slots), 1))
    mask = jnp.concatenate(masks, axis=0)
    rank = jnp.dot(mask.astype(BF16), jnp.where(before, 1.0, 0.0).astype(BF16),
                   preferred_element_type=F32)
    place = lax.broadcasted_iota(jnp.int32, (128, slots), 0).astype(F32)
    line = lax.broadcasted_iota(jnp.int32, (8, slots), 0)
    for e in range(n_row):
        chosen = jnp.where((place == rank[e:e + 1, :]) & (masks[e] > 0.5), 1.0, 0.0)
        sel[e * cap:(e + 1) * cap, :] = chosen[:cap].astype(BF16)
        local = jnp.where(masks[e] > 0.5, locals_[e], 0)
        high = jnp.right_shift(local, 6).astype(F32)
        low = jnp.bitwise_and(local, 63).astype(F32)
        parts = jnp.where(line == 0, high, jnp.where(line == 1, low, 1.0))
        got = lax.dot_general(parts.astype(BF16), chosen.astype(BF16), NT,
                              preferred_element_type=F32)
        packed = jnp.where(got[2:3] > 0.5, got[0:1] * 64.0 + got[1:2], -1.0)
        wide = jnp.broadcast_to(packed, (8, 128))
        if e == 0:
            cid_r[0] = wide
        else:
            cid_s[e] = wide

    pl.semaphore_wait(barrier, n_row - 1 + len(col_steps))
    cid_copies, q_copies = {}, {}

    def key_slot(owner):
        return kn.at[pl.ds(pl.multiple_of(owner * rows, rows), rows)]

    def key_copy(way, h):
        step = 1 if way == 0 else -1
        owner = r - step * (h - 1)
        src = emb if h == 1 else key_slot(owner)
        return remote(src, key_slot(owner), k_ss.at[way, h], k_rs.at[way, h], (r + step, c))

    def sends(way, h):
        return (r + 1 < n_row) & (r >= h - 1) if way == 0 else (r >= 1) & (r + h - 1 < n_row)

    def key_send(h):
        for way in range(2):
            @pl.when(sends(way, h))
            def _():
                key_copy(way, h).start()

    def key_sent(h):
        for way in range(2):
            @pl.when(sends(way, h))
            def _():
                key_copy(way, h).wait_send()

    def key_wait(h):
        for way in range(2):
            @pl.when((r >= h) if way == 0 else (r + h < n_row))
            def _():
                owner = r - h if way == 0 else r + h
                remote(emb, key_slot(owner), k_ss.at[way, h], k_rs.at[way, h],
                       row_peer(1)).wait_recv()

    for e in range(1, n_row):
        back = n_row - e
        cid_copies[e] = remote(cid_s.at[e], cid_r.at[back], cid_ss.at[e], cid_rs.at[back],
                               row_peer(e))
        cid_copies[e].start()
    key_send(1)
    own_rows = pl.ds(pl.multiple_of(core * rows, rows), rows)
    for m, b in col_steps:
        q_copies[m, b] = remote(emb, q.at[chip, own_rows], q_ss.at[2 * m + b],
                                q_rs.at[mirror(m, b)], col_peer(m, b))
        q_copies[m, b].start()
    kn[pl.ds(pl.multiple_of(r * rows, rows), rows), :] = emb[...]
    q[chip, own_rows, :] = emb[...]

    columns = []
    for e in range(n_row):
        if e:
            remote(cid_s.at[e], cid_r.at[e], cid_ss.at[e], cid_rs.at[e], row_peer(e)).wait_recv()
        columns.append(jnp.broadcast_to(cid_r[e][0:1, :], (128, 128)).T[:cap])
    wanted = jnp.concatenate(columns, axis=0)
    lane = lax.broadcasted_iota(jnp.int32, (n_row * cap, 128), 1).astype(F32)
    for j in range(owned // 128):
        hot[:, j * 128:(j + 1) * 128] = jnp.where(
            wanted == lane + float(j * 128), 1.0, 0.0).astype(BF16)
    load.wait()
    for j in range(D // 256):
        part = pl.ds(j * 256, 256)
        picked = jnp.dot(hot[...], idx_v[:, part], preferred_element_type=F32).astype(BF16)
        ng_r[0:cap, part] = picked[:cap]
        ng_s[:, part] = picked
    if n_row > 2:
        key_wait(1)
        key_send(2)
    ng_copies = {}
    for e in range(1, n_row):
        back = n_row - e
        ng_copies[e] = remote(ng_s.at[pl.ds(e * cap, cap)], ng_r.at[pl.ds(back * cap, cap)],
                              ng_ss.at[e], ng_rs.at[back], row_peer(e))
        ng_copies[e].start()

    for h in range(2, n_row - 1):
        key_wait(h)
        key_send(h + 1)
    for m, b in col_steps:
        at = lax.rem(chip + m, n_chip)
        half = pl.multiple_of((core if b == 0 else 1 - core) * rows, rows)
        remote(emb, q.at[at, pl.ds(half, rows)], q_ss.at[2 * m + b], q_rs.at[2 * m + b],
               col_peer(m, b)).wait_recv()

    def score(owner):
        part = pl.ds(pl.multiple_of(owner * rows, rows), rows)
        for m in range(n_chip):
            at = lax.rem(chip + m, n_chip)
            s[at, part, :] = lax.dot_general(kn[part, :], q[at], NT,
                                             preferred_element_type=F32) * scale

    def score_away(h):
        @pl.when(r >= h)
        def _():
            score(r - h)

        @pl.when(r + h < n_row)
        def _():
            score(r + h)

    score(r)
    own = lax.broadcasted_iota(jnp.int32, (rows, 2 * rows), 0)
    other = lax.broadcasted_iota(jnp.int32, (rows, 2 * rows), 1) - core * rows
    own_part = pl.ds(pl.multiple_of(r * rows, rows), rows)
    block = s[chip, own_part, :]
    positive = jnp.sum(jnp.where(jnp.bitwise_xor(own, 1) == other, block, 0.0), axis=0,
                       keepdims=True)
    s[chip, own_part, :] = jnp.where(own == other, -jnp.inf, block)
    for h in range(1, n_row):
        if h == n_row - 1:
            key_wait(h)
        score_away(h)
    own = lax.broadcasted_iota(jnp.int32, (n_key, 2 * rows), 0) - r * rows
    other = lax.broadcasted_iota(jnp.int32, (n_key, 2 * rows), 1) - core * rows
    other = jnp.where((other >= 0) & (other < rows), other, 2 * n_key)
    partner = jnp.bitwise_xor(own, 1) == other

    for e in range(1, n_row):
        remote(ng_s.at[pl.ds(e * cap, cap)], ng_r.at[pl.ds(e * cap, cap)], ng_ss.at[e],
               ng_rs.at[e], row_peer(e)).wait_recv()
    kn[n_key:n_key + slots, :] = lax.dot_general(
        sel[...], ng_r[...], TN, preferred_element_type=F32).astype(BF16)
    live = (lax.broadcasted_iota(jnp.int32, (slots, 2 * rows), 0) + c * slots) < cnt[0]
    for m in range(n_chip):
        at = lax.rem(chip + m, n_chip)
        hard = lax.dot_general(kn[n_key:n_key + slots, :], q[at], NT,
                               preferred_element_type=F32) * scale
        hard = jnp.where(live, hard, -jnp.inf)
        s[at, n_key:n_key + slots, :] = hard
        block = s[at, 0:n_key, :]
        top = jnp.maximum(jnp.max(block, axis=0, keepdims=True),
                          jnp.max(hard, axis=0, keepdims=True))
        total = (jnp.sum(jnp.exp(block - top), axis=0, keepdims=True)
                 + jnp.sum(jnp.exp(hard - top), axis=0, keepdims=True))
        st_s[at, 0:1, :] = top
        st_s[at, 1:2, :] = total
    st_copies = {}
    for m, b in col_steps:
        st_copies[m, b] = remote(st_s, st_r.at[mirror(m, b)], st_ss.at[2 * m + b],
                                 st_rs.at[mirror(m, b)], col_peer(m, b))
        st_copies[m, b].start()
    for m, b in col_steps:
        remote(st_s, st_r.at[2 * m + b], st_ss.at[2 * m + b], st_rs.at[2 * m + b],
               col_peer(m, b)).wait_recv()

    def lse_of(at):
        tops = [st_s[at, 0:1, :]] + [st_r[2 * m + b, at, 0:1, :] for m, b in col_steps]
        sums = [st_s[at, 1:2, :]] + [st_r[2 * m + b, at, 1:2, :] for m, b in col_steps]
        top = functools.reduce(jnp.maximum, tops)
        return top + jnp.log(sum(v * jnp.exp(t - top) for t, v in zip(tops, sums)))

    own_lse = lse_of(chip)
    both = jnp.concatenate([own_lse, own_lse - positive], axis=0)
    half = jnp.where(core == 0, both[:, 0:rows], both[:, rows:2 * rows])
    loss[...] = half[1:2]
    mine = jnp.broadcast_to(half[0:1], (8, rows))
    lk_s[...] = mine
    lk_r[r] = mine
    lk_copies = {}
    for e in range(1, n_row):
        lk_copies[e] = remote(lk_s, lk_r.at[r], lk_ss.at[e], lk_rs.at[n_row - e], row_peer(e))
        lk_copies[e].start()

    def query_term(m):
        at = lax.rem(chip + m, n_chip)
        weight = jnp.exp(s[at] - (own_lse if m == 0 else lse_of(at)))
        if m == 0:
            weight = jnp.concatenate(
                [weight[0:n_key] - jnp.where(partner, 1.0, 0.0), weight[n_key:]], axis=0)
        return lax.dot_general(weight.astype(BF16), kn[...], TN, preferred_element_type=F32)

    def key_term(m):
        weight = jnp.exp(s[lax.rem(chip + m, n_chip), 0:n_key, :] - key_lse)
        if m == 0:
            weight = weight - jnp.where(partner, 1.0, 0.0)
        return lax.dot_general(weight.astype(BF16), kn[0:n_key, :], TN,
                               preferred_element_type=F32)

    order = list(range(1, n_chip)) + [0]
    early = order[:2]
    for n, m in enumerate(early):
        acc[n] = query_term(m)
    key_lse = []
    for e in range(1, n_row):
        remote(lk_s, lk_r.at[lax.rem(r + e, n_row)], lk_ss.at[e], lk_rs.at[e],
               row_peer(e)).wait_recv()
    for e in range(n_row):
        key_lse.append(jnp.broadcast_to(lk_r[e][0:1, :], (rows, rows)).T)
    key_lse = jnp.concatenate(key_lse, axis=0)
    key_lse = jnp.concatenate([key_lse, key_lse], axis=1)

    sib_copies, red_copies, unit_copies = {}, {}, {}
    sibling = col_peer(0, 1)

    def pass_on(m):
        sib_copies[m].wait_recv()
        both_sum = keep[m] + sib_r[m]
        largest = jnp.maximum(jnp.max(jnp.abs(both_sum), axis=1, keepdims=True), 1e-30)
        unit = largest * (1.0 / 32000.0)
        steps = jnp.round(both_sum * (1.0 / unit))
        red_s[m] = steps.astype(jnp.int32).astype(jnp.int16)
        unit_s[m] = jnp.broadcast_to(unit, (rows, 128)).T[0:8]
        back = n_chip - m
        red_copies[m] = remote(red_s.at[m], red_r.at[back], red_ss.at[m], red_rs.at[back],
                               col_peer(m, 0))
        red_copies[m].start()
        unit_copies[m] = remote(unit_s.at[m], unit_r.at[back], unit_ss.at[m], unit_rs.at[back],
                                col_peer(m, 0))
        unit_copies[m].start()

    for n, m in enumerate(order):
        term = acc[n] + key_term(m) if m in early else query_term(m) + key_term(m)
        keep[m] = jnp.where(core == 0, term[0:rows], term[rows:])
        sib_s[m] = jnp.where(core == 0, term[rows:], term[0:rows])
        sib_copies[m] = remote(sib_s.at[m], sib_r.at[m], sib_ss.at[m], sib_rs.at[m], sibling)
        sib_copies[m].start()
        if n >= 1:
            pass_on(order[n - 1])
    sib_copies[0].wait_recv()
    total = keep[0] + sib_r[0]
    for m in range(1, n_chip):
        remote(red_s.at[m], red_r.at[m], red_ss.at[m], red_rs.at[m], col_peer(m, 0)).wait_recv()
        remote(unit_s.at[m], unit_r.at[m], unit_ss.at[m], unit_rs.at[m],
               col_peer(m, 0)).wait_recv()
        unit = jnp.broadcast_to(unit_r[m][0:1, :], (128, rows)).T[:, 0:1]
        total += red_r[m].astype(jnp.int32).astype(F32) * unit
    grad[...] = total

    for h in range(1, n_row):
        key_sent(h)
    for copies in (cid_copies, q_copies, ng_copies, st_copies, lk_copies,
                   sib_copies, red_copies, unit_copies):
        for copy in copies.values():
            copy.wait_send()


def per_device(n_row, n_col, embeddings, neg_ids, neg_counts, index_rows):
    rows = embeddings.shape[0]
    slots = neg_ids.shape[1]
    owned = index_rows.shape[0]
    cap = 2 * slots // n_row
    n_chip = n_col // 2
    n_key = n_row * rows
    vmem = pltpu.VMEM
    dma = pltpu.SemaphoreType.DMA
    loss, grad = pl.pallas_call(
        functools.partial(kernel, n_row, n_col, cap),
        out_shape=(jax.ShapeDtypeStruct((1, rows), F32),
                   jax.ShapeDtypeStruct((rows, D), F32)),
        in_specs=[pl.BlockSpec(memory_space=vmem), pl.BlockSpec(memory_space=vmem),
                  pl.BlockSpec(memory_space=pltpu.SMEM), pl.BlockSpec(memory_space=pl.ANY)],
        out_specs=(pl.BlockSpec(memory_space=vmem), pl.BlockSpec(memory_space=vmem)),
        scratch_shapes=[
            vmem((n_chip, 2 * rows, D), BF16),
            vmem((n_key + slots, D), BF16),
            vmem((n_chip, n_key + slots, 2 * rows), F32),
            vmem((n_row * cap, slots), BF16),
            vmem((n_row, 8, 128), F32),
            vmem((n_row, 8, 128), F32),
            vmem((owned, D), BF16),
            vmem((n_row * cap, owned), BF16),
            vmem((n_row * cap, D), BF16),
            vmem((n_row * cap, D), BF16),
            vmem((n_chip, 2, 2 * rows), F32),
            vmem((n_col, n_chip, 2, 2 * rows), F32),
            vmem((8, rows), F32),
            vmem((n_row, 8, rows), F32),
            vmem((n_chip, rows, D), F32),
            vmem((n_chip, rows, D), F32),
            vmem((n_chip, rows, D), F32),
            vmem((n_chip, rows, D), jnp.int16),
            vmem((n_chip, rows, D), jnp.int16),
            vmem((n_chip, 8, rows), F32),
            vmem((n_chip, 8, rows), F32),
            vmem((2, 2 * rows, D), F32),
            dma,
            dma((n_row,)), dma((n_row,)), dma((2, n_row)), dma((2, n_row)),
            dma((n_col,)), dma((n_col,)), dma((n_row,)), dma((n_row,)),
            dma((n_col,)), dma((n_col,)), dma((n_row,)), dma((n_row,)),
            dma((n_chip,)), dma((n_chip,)), dma((n_chip,)), dma((n_chip,)),
            dma((n_chip,)), dma((n_chip,)),
        ],
        compiler_params=pltpu.CompilerParams(
            collective_id=0, has_side_effects=True, vmem_limit_bytes=58 * 1024 * 1024),
    )(embeddings, neg_ids, neg_counts, index_rows)
    return loss.reshape(rows), grad


def solution(mesh):
    return jax.shard_map(
        functools.partial(per_device, mesh.shape["row"], mesh.shape["col"]),
        mesh=mesh,
        in_specs=(P(("row", "col"), None), P("row", "col"), P("row"), P("row", None)),
        out_specs=(P(("row", "col")), P(("row", "col"), None)),
        check_vma=False,
    )
```
